256 devices in a mesh: dp: 16 (over x, y), ctx: 16 (over z, core).
Axes of the slice: x: 4, y: 4, z: 8, core: 2. Of those that a mesh axis runs over, the one named last changes fastest.
Arguments:
- queries: bfloat16 [16, 4096, 512], P('dp', 'ctx'), may hold values from -125 to 125
- key_rows: bfloat16 [16, 4096, 128], P('dp', 'ctx'), may hold values from -5.75 to 5.75
- value_rows: bfloat16 [16, 4096, 128], P('dp', 'ctx'), may hold values from -6 to 6
- out_grad: bfloat16 [16, 4096, 512], P('dp', 'ctx'), may hold values from -0.0234375 to 0.0234375
- inputs: bfloat16 [16, 4096, 16384], P('dp', 'ctx'), may hold values from -8 to 8
- pair_order: int32 [16], replicated, may hold values from 0 to 15, each once
Outputs:
- attention: bfloat16 [16, 4096, 512], P('dp', 'ctx')
- weight_grads: float32 [16384, 768], P('ctx')
The draws below stay inside these ranges and needn't reach their ends.
Inputs may be any that keep to these rules, and one draw needn't show every extreme that they name: Index c of ctx holds segments pair_order[c] (its first 128 rows) and 31-pair_order[c] (the rest), each of 128 tokens.
All inputs are finite; a program needn't handle non-finite values.
Results may differ from the reference program's by a relative error of at most 0.028.
Values may be sent and summed in bfloat16 or wider, within the bound.
No kernel may reach another device: no remote copies, remote signals or barrier semaphores. Data moves between devices by JAX's collectives and lax.ppermute only.
A program may use at most 192 MiB of HBM per device.

```python
import math
import jax
import jax.numpy as jnp
from jax import lax

D = 16384
HEAD = 128
QHEADS = 4
TOK_DEV = 256
SEQ = 4096
BATCH = 16
COLS = 768
N_DP = 16
N_CTX = 16


def shared_base(key):
    return jnp.clip(jax.random.normal(key, (BATCH, SEQ, HEAD), jnp.float32), -5.0, 5.0)


def draw_key_rows(key, part):
    base_rows = shared_base(key)
    result = base_rows
    return result.astype(jnp.bfloat16)


def draw_queries(key, part):
    key = jax.random.fold_in(key, 12)
    first_key = jax.random.fold_in(key, 0)
    result = jnp.clip(jax.random.normal(first_key, (BATCH, SEQ, QHEADS * HEAD), jnp.float32), -5.0, 5.0)
    return result.astype(jnp.bfloat16)


def raised(entries, stream_key, source, target, parts, factor):
    owner, partner = [(jnp.arange(entries.shape[position]) // (entries.shape[position] // parts)).reshape([-1 if axis == position else 1 for axis in range(entries.ndim)]) for position in (source, target)]
    chosen = jax.random.permutation(stream_key, parts)[partner]
    strong = (owner == chosen) | (owner == (partner + parts // 2) % parts)
    return jnp.where(strong, factor * entries, entries)


def block_scale(rng, extent, cuts, least, largest):
    loudness = 1.0
    for axis_at, parts in cuts:
        heights = jax.random.uniform(jax.random.fold_in(jax.random.fold_in(rng, 6), axis_at), (parts,), jnp.float32, least / len(cuts), largest / len(cuts))
        loudness = loudness * jnp.repeat(jnp.exp(heights), extent[axis_at] // parts).reshape((-1,) + (1,) * (len(extent) - 1 - axis_at))
    return loudness


def scatter_about(own_key, extent, deviation, most, pieces=(), held_as=jnp.bfloat16):
    values = deviation * jax.random.normal(own_key, extent, jnp.float32)
    if pieces:
        values = values * block_scale(own_key, extent, pieces, -0.22, 0.18)
    return jnp.clip(values, -most, most).astype(held_as)


def noise_with(stream_key, dims, width, reach, cuts, heavy, kind=jnp.bfloat16):
    array = width * jax.random.normal(stream_key, dims, jnp.float32)
    if cuts:
        array = array * block_scale(stream_key, dims, cuts, -0.22, 0.18)
    return jnp.clip(raised(array, jax.random.fold_in(stream_key, 3), *heavy), -reach, reach).astype(kind)


def setup_inputs(seed: int = 0) -> dict:
    key_list = jax.random.split(jax.random.key(seed), 7)
    return {
        "queries": draw_queries(jax.random.fold_in(key_list[6], 71), 0),
        "key_rows": draw_key_rows(jax.random.fold_in(key_list[6], 71), 0),
        "value_rows": scatter_about(key_list[2], (BATCH, SEQ, HEAD), 1.0, 6.0, ((0, 16), (1, 16))),
        "out_grad": scatter_about(key_list[3], (BATCH, SEQ, QHEADS * HEAD), ((N_DP * SEQ) ** -0.5), 0.0234375, ((0, 16), (1, 16))),
        "inputs": noise_with(key_list[4], (BATCH, SEQ, D), 1.0, 8.0, ((0, 16), (1, 16)), (1, 2, 16, 2.0)),
        "pair_order": jax.random.permutation(key_list[5], N_CTX).astype(jnp.int32),
    }


def positions(pair_order):
    half_rows = TOK_DEV // 2
    first_seg = pair_order.astype(jnp.int32)
    segments = jnp.stack([first_seg, 2 * N_CTX - 1 - first_seg], axis=1)
    offsets = jnp.arange(half_rows, dtype=jnp.int32)
    return (segments[:, :, None] * half_rows + offsets[None, None, :]).reshape(-1)

def block_grads(query_blk, query_pos, key_all, value_all, key_pos, grad_blk):
    score_scale = 1.0 / math.sqrt(HEAD)
    query_heads = query_blk.reshape(TOK_DEV, QHEADS, HEAD).astype(jnp.float32)
    grad_heads = grad_blk.reshape(TOK_DEV, QHEADS, HEAD).astype(jnp.float32)
    key_wide = key_all.astype(jnp.float32)
    value_wide = value_all.astype(jnp.float32)
    scores = jnp.einsum('thd,kd->htk', query_heads, key_wide) * score_scale
    visible = key_pos[None, None, :] <= query_pos[None, :, None]
    scores = jnp.where(visible, scores, -jnp.inf)
    row_max = lax.optimization_barrier(jnp.max(scores, axis=-1, keepdims=True))
    unnorm = jnp.exp(scores - row_max)
    probs = (unnorm / lax.optimization_barrier(jnp.sum(unnorm, axis=-1, keepdims=True))).astype(jnp.bfloat16)
    prob_wide = probs.astype(jnp.float32)
    attn_rows = jnp.einsum('htk,kd->thd', prob_wide, value_wide).astype(jnp.bfloat16)
    prob_grads = jnp.einsum('thd,kd->htk', grad_heads, value_wide)
    row_terms = lax.optimization_barrier(jnp.sum(grad_heads * attn_rows.astype(jnp.float32), axis=-1))
    score_grads = (prob_wide * (prob_grads - row_terms.T[:, :, None])).astype(jnp.bfloat16)
    grads_wide = score_grads.astype(jnp.float32)
    query_grads = (jnp.einsum('htk,kd->thd', grads_wide, key_wide) * score_scale).astype(jnp.bfloat16)
    key_terms = (jnp.einsum('htk,thd->kd', grads_wide, query_heads) * score_scale).astype(jnp.bfloat16)
    value_terms = jnp.einsum('htk,thd->kd', prob_wide, grad_heads).astype(jnp.bfloat16)
    return (attn_rows.reshape(TOK_DEV, -1), query_grads.reshape(TOK_DEV, -1), key_terms, value_terms)

def reference(queries, key_rows, value_rows, out_grad, inputs, pair_order):
    token_pos = positions(pair_order)
    block_pos = token_pos.reshape(N_CTX, TOK_DEV)

    def per_sequence(running, slices):
        seq_queries, seq_keys, seq_values, seq_grads, seq_inputs = slices
        query_blocks = seq_queries.reshape(N_CTX, TOK_DEV, -1)
        grad_blocks = seq_grads.reshape(N_CTX, TOK_DEV, -1)

        def per_block(sums_now, block_items):
            query_blk, grad_blk, query_pos = block_items
            attn_rows, query_grads, key_terms, value_terms = block_grads(query_blk, query_pos, seq_keys, seq_values, token_pos, grad_blk)
            return ((sums_now[0] + key_terms.astype(jnp.float32), sums_now[1] + value_terms.astype(jnp.float32)), (attn_rows, query_grads))
        empty_sums = jnp.zeros((SEQ, HEAD), jnp.float32)
        (key_sum, value_sum), (attn_blocks, query_blocks_grad) = lax.scan(per_block, (empty_sums, empty_sums), (query_blocks, grad_blocks, block_pos))
        token_grads = jnp.concatenate([query_blocks_grad.reshape(SEQ, -1), key_sum.astype(jnp.bfloat16), value_sum.astype(jnp.bfloat16)], axis=1)
        running = running + jnp.dot(seq_inputs.T, token_grads, preferred_element_type=jnp.float32)
        return (running, attn_blocks.reshape(SEQ, -1))
    start_sums = jnp.zeros((D, COLS), jnp.float32)
    weight_grads, attention = lax.scan(per_sequence, start_sums, (queries, key_rows, value_rows, out_grad, inputs))
    return (attention, weight_grads)
```

```python
import functools
import math

import jax
import jax.numpy as jnp
from jax import lax
from jax.experimental import pallas as pl
from jax.experimental.pallas import tpu as pltpu
from jax.sharding import PartitionSpec as P

TOK = 256
HALF = 128
HEAD = 128
HEADS = 4
ROWS = HEADS * HALF
NZ = 8
BF = jnp.bfloat16
F32 = jnp.float32
SCALE = 1.0 / math.sqrt(HEAD)
VMEM = 56 * 1024 * 1024

CORE = [(i, i ^ 1) for i in range(16)]


def z_shift(step):
    return [(i, (i + 2 * step) % 16) for i in range(16)]


def x_shift(step):
    return [(i, ((i // 4 + step) % 4) * 4 + i % 4) for i in range(16)]


def y_shift(step):
    return [(i, (i // 4) * 4 + (i % 4 + step) % 4) for i in range(16)]


SHIFTS = (x_shift, y_shift)


def dot(a, b, ca, cb):
    return lax.dot_general(a, b, (((ca,), (cb,)), ((), ())), preferred_element_type=F32)


def attention_kernel(me_ref, order_ref, q_ref, g_ref, *refs):
    kv_refs, refs = refs[:16], refs[16:]
    attn_ref, qg_ref, keep_ref, send_ref = refs[:4]
    kv, qs, gs, st, mb, lv, acc, rt, sems = refs[4:]
    me = me_ref[0]
    my_z, my_core = me // 2, me % 2
    own = order_ref[me]
    copies = [pltpu.make_async_copy(kv_refs[r], kv.at[r], sems.at[r]) for r in range(16)]
    for copy in copies:
        copy.start()
    for a in range(2):
        for h in range(HEADS):
            rows, cols = pl.ds(a * HALF, HALF), pl.ds(h * HEAD, HEAD)
            qs[a, pl.ds(h * HALF, HALF), :] = q_ref[rows, cols]
            gs[a, pl.ds(h * HALF, HALF), :] = g_ref[rows, cols]
    for copy in copies:
        copy.wait()

    def upper(r):
        src = 2 * ((my_z + r % NZ) % NZ) + (my_core + r // NZ) % 2
        return (order_ref[src] > own).astype(jnp.int32)

    def keys(r, half):
        return kv[r, pl.ds(pl.multiple_of(half * HALF, HALF), HALF), :HEAD]

    def values(r, half):
        return kv[r, pl.ds(pl.multiple_of(half * HALF, HALF), HALF), HEAD:]

    causal = (
        lax.broadcasted_iota(jnp.int32, (ROWS, HALF), 0) % HALF
        >= lax.broadcasted_iota(jnp.int32, (ROWS, HALF), 1)
    )

    def score(a, r, half):
        return dot(qs[a], keys(r, half), 1, 1) * SCALE

    s0 = score(1, 0, 0)
    s1 = jnp.where(causal, score(0, 0, 0), -jnp.inf)
    s2 = jnp.where(causal, score(1, 0, 1), -jnp.inf)
    st[0], st[1], st[32] = s0, s1, s2
    mb[0], mb[1] = s1, jnp.maximum(s0, s2)

    def score_step(r, carry):
        a = upper(r)
        t0 = score(1, r, 0)
        st[2 * r] = t0
        mb[1] = jnp.maximum(mb[1], t0)
        t1 = score(a, r, a)
        st[2 * r + 1] = t1
        mb[a] = jnp.maximum(mb[a], t1)
        return carry

    lax.fori_loop(1, 16, score_step, 0)
    for a in range(2):
        mb[a] = jnp.broadcast_to(jnp.max(mb[a], axis=1, keepdims=True), (ROWS, HEAD))
        lv[a] = jnp.zeros((ROWS, HEAD), F32)
        acc[a] = jnp.zeros((ROWS, HEAD), F32)

    def forward_tile(tile, a, r, half):
        unnorm = jnp.exp(st[tile] - mb[a])
        st[tile] = unnorm
        lv[a] += unnorm
        acc[a] += dot(unnorm.astype(BF), values(r, half), 1, 0)

    forward_tile(32, 1, 0, 1)

    def forward_step(r, carry):
        a = jnp.where(r == 0, 0, upper(r))
        forward_tile(2 * r, 1, r, 0)
        forward_tile(2 * r + 1, a, r, a)
        return carry

    lax.fori_loop(0, 16, forward_step, 0)
    for a in range(2):
        inv = 1.0 / jnp.sum(lv[a], axis=1, keepdims=True)
        out = (acc[a] * inv).astype(BF)
        terms = jnp.sum(gs[a].astype(F32) * out.astype(F32), axis=1, keepdims=True)
        lv[a] = jnp.broadcast_to(inv, (ROWS, HEAD))
        rt[a] = jnp.broadcast_to(terms, (ROWS, HEAD))
        acc[a] = jnp.zeros((ROWS, HEAD), F32)
        for h in range(HEADS):
            attn_ref[pl.ds(a * HALF, HALF), pl.ds(h * HEAD, HEAD)] = out[h * HALF : (h + 1) * HALF]

    def backward_tile(tile, a, r, half):
        probs = st[tile] * lv[a]
        prob_grads = dot(gs[a], values(r, half), 1, 1)
        grads = (probs * (prob_grads - rt[a])).astype(BF)
        acc[a] += dot(grads, keys(r, half), 1, 0)
        key_term = dot(grads, qs[a], 0, 0) * SCALE
        value_term = dot(probs.astype(BF), gs[a], 0, 0)
        return jnp.concatenate([key_term, value_term], axis=1)

    low = backward_tile(0, 1, 0, 0) + backward_tile(1, 0, 0, 0)
    keep_ref[0, :HALF, :] = low.astype(BF)
    keep_ref[0, HALF:, :] = backward_tile(32, 1, 0, 1).astype(BF)

    def backward_step(out_ref, flip, dz, carry):
        r = flip * NZ + dz
        a = upper(r)
        t0 = backward_tile(2 * r, 1, r, 0)
        t1 = backward_tile(2 * r + 1, a, r, a)
        out_ref[dz, :HALF, :] = (t0 + jnp.where(a == 0, t1, 0.0)).astype(BF)
        out_ref[dz, HALF:, :] = jnp.where(a == 1, t1, 0.0).astype(BF)
        return carry

    lax.fori_loop(0, NZ, functools.partial(backward_step, send_ref, 1), 0)
    lax.fori_loop(1, NZ, functools.partial(backward_step, keep_ref, 0), 0)
    for a in range(2):
        for h in range(HEADS):
            qg_ref[pl.ds(a * HALF, HALF), pl.ds(h * HEAD, HEAD)] = (
                acc[a, pl.ds(h * HALF, HALF), :] * SCALE
            ).astype(BF)


def attention(me, order, queries, out_grad, blocks):
    smem = pl.BlockSpec(memory_space=pltpu.SMEM)
    vmem = pl.BlockSpec(memory_space=pltpu.VMEM)
    hbm = pl.BlockSpec(memory_space=pl.ANY)
    wide = jax.ShapeDtypeStruct((TOK, HEADS * HEAD), BF)
    terms = jax.ShapeDtypeStruct((NZ, TOK, 2 * HEAD), BF)
    stat = pltpu.VMEM((2, ROWS, HEAD), F32)
    return pl.pallas_call(
        attention_kernel,
        in_specs=[smem, smem, vmem, vmem] + [hbm] * 16,
        out_specs=[vmem] * 4,
        out_shape=[wide, wide, terms, terms],
        scratch_shapes=[
            pltpu.VMEM((16, TOK, 2 * HEAD), BF),
            pltpu.VMEM((2, ROWS, HEAD), BF),
            pltpu.VMEM((2, ROWS, HEAD), BF),
            pltpu.VMEM((33, ROWS, HALF), F32),
            stat,
            stat,
            stat,
            stat,
            pltpu.SemaphoreType.DMA((16,)),
        ],
        compiler_params=pltpu.CompilerParams(vmem_limit_bytes=VMEM),
        cost_estimate=pl.CostEstimate(
            flops=12 * 33 * ROWS * HALF * HEAD, bytes_accessed=6 * 2**20, transcendentals=33 * ROWS * HALF
        ),
        name="attention",
    )(me, order, queries, out_grad, *blocks)


def pack_kernel(meta_ref, *refs):
    del meta_ref
    count = len(refs) * 2 // 3
    for n in range(count // 2):
        for j in range(2):
            refs[count + n][j] = refs[2 * n + j][...]


def pack(meta, inputs, wanted):
    def column(axis, step, j):
        def index(z, meta_ref):
            c = 2 * z + (meta_ref[2] + j) % 2
            return (0, c * 8 + axis * 4 + (meta_ref[axis] + step) % 4)

        return pl.BlockSpec((TOK, 128), index)

    return pl.pallas_call(
        pack_kernel,
        grid_spec=pltpu.PrefetchScalarGridSpec(
            num_scalar_prefetch=1,
            grid=(NZ,),
            in_specs=[column(axis, step, j) for axis, step in wanted for j in range(2)],
            out_specs=[pl.BlockSpec((2, TOK, 128), lambda z, m: (0, 0, z))] * len(wanted),
        ),
        out_shape=[jax.ShapeDtypeStruct((2, TOK, 128 * NZ), BF)] * len(wanted),
        cost_estimate=pl.CostEstimate(flops=0, bytes_accessed=len(wanted) * 2**21, transcendentals=0),
        name="pack",
    )(meta, *([inputs] * (2 * len(wanted))))


def product_kernel(other, meta_ref, *refs):
    tokens, grads, outs, acc = refs[:8], refs[8:16], refs[16:20], refs[20]
    total = dot(tokens[0][...], grads[0][...], 0, 0)
    for n in range(1, 8):
        total += dot(tokens[n][...], grads[n][...], 0, 0)
    acc[...] = total
    for step in range(4):
        part = (meta_ref[other] + step) % 4
        for z in range(2):
            start = pl.multiple_of(z * 128 + part * 32, 32)
            outs[step][z] = acc[pl.ds(start, 32), :].astype(BF)


def product(meta, axis, tokens, grads):
    cols = grads[0].shape[1]
    return pl.pallas_call(
        functools.partial(product_kernel, 1 - axis),
        grid_spec=pltpu.PrefetchScalarGridSpec(
            num_scalar_prefetch=1,
            grid=(4,),
            in_specs=[pl.BlockSpec((TOK, 256), lambda i, m: (0, i))] * 8
            + [pl.BlockSpec((TOK, cols), lambda i, m: (0, 0))] * 8,
            out_specs=[pl.BlockSpec((2, 32, cols), lambda i, m: (i, 0, 0))] * 4,
            scratch_shapes=[pltpu.VMEM((256, cols), F32)],
        ),
        out_shape=[jax.ShapeDtypeStruct((NZ, 32, cols), BF)] * 4,
        compiler_params=pltpu.CompilerParams(vmem_limit_bytes=VMEM),
        cost_estimate=pl.CostEstimate(
            flops=2 * 2048 * 1024 * cols, bytes_accessed=4 * 2**20 + 6144 * cols, transcendentals=0
        ),
        name="product",
    )(meta, *tokens, *grads)


def total(parts):
    out = parts[0].astype(F32)
    for part in parts[1:]:
        out = out + part.astype(F32)
    return out


def swap(a):
    return lax.ppermute(a, "ctx", CORE)


def send(a, axis, step):
    return lax.ppermute(a, "dp", SHIFTS[axis](step))


STEPS = (2, 1, 3)


def share_tokens(grads):
    own, mate = grads, swap(grads)
    got = {(axis, step): send(grads, axis, step) for step in STEPS for axis in range(2)}
    return [
        [own, mate] + [t for step in STEPS for t in (got[axis, step], swap(got[axis, step]))] for axis in range(2)
    ]


def column_sums(meta, tokens, grads):
    shared = share_tokens(grads)
    sums = []
    for axis in range(2):
        parts = product(meta, axis, tokens[axis], shared[axis])
        sums.append(total([parts[0]] + [send(parts[step], 1 - axis, step) for step in STEPS]).astype(BF))
    return jnp.concatenate(sums, axis=1)


def per_device(queries, key_rows, value_rows, out_grad, inputs, pair_order):
    ctx, dp = lax.axis_index("ctx"), lax.axis_index("dp")
    meta = jnp.stack([dp // 4, dp % 4, ctx % 2, ctx]).astype(jnp.int32)
    me = ctx.reshape(1).astype(jnp.int32)
    own = jnp.concatenate([key_rows[0], value_rows[0]], axis=1)

    blocks = [None] * 16
    blocks[0], blocks[8] = own, swap(own)
    up = down = own
    for s in range(1, 5):
        up = lax.ppermute(up, "ctx", z_shift(1))
        blocks[8 - s], blocks[16 - s] = up, swap(up)
        if s < 4:
            down = lax.ppermute(down, "ctx", z_shift(-1))
            blocks[s], blocks[8 + s] = down, swap(down)

    far = pack(meta, inputs[0], [(0, 2), (1, 2)])
    near = pack(meta, inputs[0], [(0, 1), (0, 3), (1, 1), (1, 3), (0, 0), (1, 0)])
    packed = {(0, 2): far[0], (1, 2): far[1], (0, 1): near[0], (0, 3): near[1], (1, 1): near[2], (1, 3): near[3]}
    got = {key: send(part, *key) for key, part in packed.items()}
    tokens = [
        [t for part in [near[4 + axis]] + [got[axis, step] for step in STEPS] for t in (part[0], swap(part[1]))]
        for axis in range(2)
    ]

    attn, query_grads, keep, give = attention(me, pair_order, queries[0], out_grad[0], blocks)

    pair = (keep.astype(F32) + swap(give).astype(F32)).astype(BF)
    pair = jnp.roll(pair, ctx // 2, axis=0)
    z_groups = [[k + 2 * z for z in range(NZ)] for k in range(2)]
    all_z = functools.partial(
        lax.all_to_all, axis_name="ctx", split_axis=0, concat_axis=0, axis_index_groups=z_groups
    )
    kv_grads = jnp.sum(all_z(pair).astype(F32), axis=0).astype(BF)

    q_sums = column_sums(meta, tokens, query_grads)
    kv_sums = column_sums(meta, tokens, kv_grads)
    mine = jnp.concatenate([q_sums, kv_sums], axis=2)
    mine = jnp.sum(all_z(mine).astype(F32), axis=0).astype(BF)
    every = lax.all_to_all(
        jnp.broadcast_to(mine[None], (16,) + mine.shape), "dp", split_axis=0, concat_axis=0
    ).astype(F32)
    first = every[:, :32].reshape(512, -1)
    second = every[:, 32:].reshape(4, 4, 32, -1).swapaxes(0, 1).reshape(512, -1)
    return attn[None], jnp.concatenate([first, second], axis=0)


def solution(mesh):
    rows = P("dp", "ctx", None)
    return jax.shard_map(
        per_device,
        mesh=mesh,
        in_specs=(rows, rows, rows, rows, rows, P()),
        out_specs=(rows, P("ctx", None)),
        check_vma=False,
    )
```

```python
import functools
import math

import jax
import jax.numpy as jnp
from jax import lax
from jax.experimental import pallas as pl
from jax.experimental.pallas import tpu as pltpu
from jax.sharding import PartitionSpec as P

TOK = 256
HALF = 128
HEAD = 128
HEADS = 4
ROWS = HEADS * HALF
NZ = 8
BF = jnp.bfloat16
F32 = jnp.float32
SCALE = 1.0 / math.sqrt(HEAD)
VMEM = 56 * 1024 * 1024

CORE = [(i, i ^ 1) for i in range(16)]


def z_shift(step):
    return [(i, (i + 2 * step) % 16) for i in range(16)]


def x_shift(step):
    return [(i, ((i // 4 + step) % 4) * 4 + i % 4) for i in range(16)]


def y_shift(step):
    return [(i, (i // 4) * 4 + (i % 4 + step) % 4) for i in range(16)]


SHIFTS = (x_shift, y_shift)


def dot(a, b, ca, cb):
    return lax.dot_general(a, b, (((ca,), (cb,)), ((), ())), preferred_element_type=F32)


BLOCK_ORDER = ((0, 1, 7, 2, 6), (3, 5, 4))


def attention_kernel(me_ref, order_ref, q_ref, g_ref, *refs):
    kv_refs, refs = refs[:4], refs[4:]
    attn_ref, qg_ref, keep_ref, send_ref = refs[:4]
    kv, qs, gs, qt, gt, st, extra, mb, lv, acc, rt, sems = refs[4:]
    me = me_ref[0]
    my_z, my_core = me // 2, me % 2
    own = order_ref[me]
    places = [(n, i, dz) for n, order in enumerate(BLOCK_ORDER) for i, dz in enumerate(order)]
    copies = [
        pltpu.make_async_copy(kv_refs[2 * flip + n].at[i], kv.at[NZ * flip + dz], sems.at[flip, dz])
        for flip in range(2)
        for n, i, dz in places
    ]
    for copy in copies:
        copy.start()
    for a in range(2):
        for h in range(HEADS):
            rows, cols, part = pl.ds(a * HALF, HALF), pl.ds(h * HEAD, HEAD), pl.ds(h * HALF, HALF)
            qs[a, part, :] = q_ref[rows, cols]
            gs[a, part, :] = g_ref[rows, cols]
            qt[a, :, part] = q_ref[rows, cols].astype(F32).T.astype(BF)
            gt[a, :, part] = g_ref[rows, cols].astype(F32).T.astype(BF)
    for copy in copies:
        copy.wait()

    def upper(r):
        src = 2 * ((my_z + r % NZ) % NZ) + (my_core + r // NZ) % 2
        return (order_ref[src] > own).astype(jnp.int32)

    def keys(r, half):
        return kv[r, pl.ds(pl.multiple_of(half * HALF, HALF), HALF), :HEAD]

    def values(r, half):
        return kv[r, pl.ds(pl.multiple_of(half * HALF, HALF), HALF), HEAD:]

    def low_keys(dz):
        return jnp.concatenate([keys(dz, 0), keys(NZ + dz, 0)], axis=0)

    def low_values(dz):
        return jnp.concatenate([values(dz, 0), values(NZ + dz, 0)], axis=0)

    def second(dz):
        return ((2, jnp.where(dz == 0, 0, upper(dz)), dz), (3, upper(NZ + dz), NZ + dz))

    causal = (
        lax.broadcasted_iota(jnp.int32, (ROWS, HALF), 0) % HALF
        >= lax.broadcasted_iota(jnp.int32, (ROWS, HALF), 1)
    )
    left, right = pl.ds(0, HALF), pl.ds(HALF, HALF)
    own_high = jnp.where(causal, dot(qs[1], keys(0, 1), 1, 1) * SCALE, -jnp.inf)
    extra[...] = own_high
    mb[0] = jnp.full((ROWS, HEAD), -jnp.inf, F32)
    mb[1] = own_high

    def score_step(dz, carry):
        t0 = dot(qs[1], low_keys(dz), 1, 1) * SCALE
        st[dz, 0], st[dz, 1] = t0[:, :HALF], t0[:, HALF:]
        mb[1] = jnp.maximum(mb[1], jnp.maximum(t0[:, :HALF], t0[:, HALF:]))
        for slot, a, r in second(dz):
            t1 = dot(qs[a], keys(r, a), 1, 1) * SCALE
            if slot == 2:
                t1 = jnp.where(jnp.logical_or(causal, dz > 0), t1, -jnp.inf)
            st[dz, slot] = t1
            mb[a] = jnp.maximum(mb[a], t1)
        return carry

    lax.fori_loop(0, NZ, score_step, 0)
    for a in range(2):
        mb[a] = jnp.broadcast_to(jnp.max(mb[a], axis=1, keepdims=True), (ROWS, HEAD))
    unnorm = jnp.exp(extra[...] - mb[1])
    extra[...] = unnorm
    lv[0] = jnp.zeros((ROWS, HEAD), F32)
    lv[1] = unnorm
    acc[0] = jnp.zeros((ROWS, HEAD), F32)
    acc[1] = dot(unnorm.astype(BF), values(0, 1), 1, 0)

    def forward_step(dz, carry):
        u0 = jnp.exp(st[dz, 0] - mb[1])
        u1 = jnp.exp(st[dz, 1] - mb[1])
        st[dz, 0], st[dz, 1] = u0, u1
        lv[1] += u0 + u1
        acc[1] += dot(jnp.concatenate([u0, u1], axis=1).astype(BF), low_values(dz), 1, 0)
        for slot, a, r in second(dz):
            unnorm = jnp.exp(st[dz, slot] - mb[a])
            st[dz, slot] = unnorm
            lv[a] += unnorm
            acc[a] += dot(unnorm.astype(BF), values(r, a), 1, 0)
        return carry

    lax.fori_loop(0, NZ, forward_step, 0)
    for a in range(2):
        inv = 1.0 / jnp.sum(lv[a], axis=1, keepdims=True)
        out = (acc[a] * inv).astype(BF)
        terms = jnp.sum(gs[a].astype(F32) * out.astype(F32), axis=1, keepdims=True)
        lv[a] = jnp.broadcast_to(inv, (ROWS, HEAD))
        rt[a] = jnp.broadcast_to(terms, (ROWS, HEAD))
        for h in range(HEADS):
            attn_ref[pl.ds(a * HALF, HALF), pl.ds(h * HEAD, HEAD)] = out[h * HALF : (h + 1) * HALF]

    def tile_grads(unnorm, a, r, half):
        probs = unnorm * lv[a]
        prob_grads = dot(gs[a], values(r, half), 1, 1)
        grads = (probs * (prob_grads - rt[a])).astype(BF)
        key_term = dot(qt[a], grads, 1, 0) * SCALE
        value_term = dot(gt[a], probs.astype(BF), 1, 0)
        return grads, jnp.concatenate([key_term, value_term], axis=0)

    grads, high_term = tile_grads(extra[...], 1, 0, 1)
    acc[0] = jnp.zeros((ROWS, HEAD), F32)
    acc[1] = dot(grads, keys(0, 1), 1, 0)
    extra[pl.ds(0, 2 * HEAD), :] = high_term

    def backward_step(dz, carry):
        inv = lv[1]
        terms = rt[1]
        p0, p1 = st[dz, 0] * inv, st[dz, 1] * inv
        prob_grads = dot(gs[1], low_values(dz), 1, 1)
        g0 = p0 * (prob_grads[:, :HALF] - terms)
        g1 = p1 * (prob_grads[:, HALF:] - terms)
        grads = jnp.concatenate([g0, g1], axis=1).astype(BF)
        probs = jnp.concatenate([p0, p1], axis=1).astype(BF)
        acc[1] += dot(grads, low_keys(dz), 1, 0)
        low = jnp.concatenate([dot(qt[1], grads, 1, 0) * SCALE, dot(gt[1], probs, 1, 0)], axis=0)
        for slot, a, r in second(dz):
            grads, term = tile_grads(st[dz, slot], a, r, a)
            acc[a] += dot(grads, keys(r, a), 1, 0)
            out_ref = keep_ref if slot == 2 else send_ref
            here = low[:, :HALF] if slot == 2 else low[:, HALF:]
            above = jnp.where(a == 1, term, 0.0)
            if slot == 2:
                above = jnp.where(dz == 0, extra[pl.ds(0, 2 * HEAD), :], above)
            out_ref[dz, :, left] = (here + jnp.where(a == 0, term, 0.0)).astype(BF)
            out_ref[dz, :, right] = above.astype(BF)
        return carry

    lax.fori_loop(0, NZ, backward_step, 0)
    for a in range(2):
        for h in range(HEADS):
            grad = acc[a, pl.ds(h * HALF, HALF), :] * SCALE
            qg_ref[pl.ds(h * HEAD, HEAD), pl.ds(a * HALF, HALF)] = grad.T.astype(BF)


def attention(me, order, queries, out_grad, blocks):
    smem = pl.BlockSpec(memory_space=pltpu.SMEM)
    vmem = pl.BlockSpec(memory_space=pltpu.VMEM)
    hbm = pl.BlockSpec(memory_space=pl.ANY)
    terms = jax.ShapeDtypeStruct((NZ, 2 * HEAD, TOK), BF)
    stat = pltpu.VMEM((2, ROWS, HEAD), F32)
    return pl.pallas_call(
        attention_kernel,
        in_specs=[smem, smem, vmem, vmem] + [hbm] * 4,
        out_specs=[vmem] * 4,
        out_shape=[
            jax.ShapeDtypeStruct((TOK, HEADS * HEAD), BF),
            jax.ShapeDtypeStruct((HEADS * HEAD, TOK), BF),
            terms,
            terms,
        ],
        scratch_shapes=[
            pltpu.VMEM((16, TOK, 2 * HEAD), BF),
            pltpu.VMEM((2, ROWS, HEAD), BF),
            pltpu.VMEM((2, ROWS, HEAD), BF),
            pltpu.VMEM((2, HEAD, ROWS), BF),
            pltpu.VMEM((2, HEAD, ROWS), BF),
            pltpu.VMEM((NZ, 4, ROWS, HALF), F32),
            pltpu.VMEM((ROWS, HALF), F32),
            stat,
            stat,
            stat,
            stat,
            pltpu.SemaphoreType.DMA((2, NZ)),
        ],
        compiler_params=pltpu.CompilerParams(vmem_limit_bytes=VMEM),
        cost_estimate=pl.CostEstimate(
            flops=22 * 10**9, bytes_accessed=6 * 2**20, transcendentals=33 * ROWS * HALF
        ),
        name="attention",
    )(me, order, queries, out_grad, *blocks)


def pack_kernel(wanted, meta_ref, in_ref, *refs):
    outs, (held, in_sems, out_sems) = refs[:-3], refs[-3:]
    reads = []
    for n, group in enumerate(wanted):
        reads.append([])
        for half, (axis, step, flip) in enumerate(group):
            core = (meta_ref[2] + flip) % 2
            part = (meta_ref[axis] + step) % 4
            for z in range(NZ):
                start = pl.multiple_of((2 * z + core) * 1024 + axis * 512 + part * 128, 128)
                copy = pltpu.make_async_copy(
                    in_ref.at[:, pl.ds(start, 128)],
                    held.at[n, half, :, pl.ds(z * 128, 128)],
                    in_sems.at[n, half, z],
                )
                copy.start()
                reads[n].append(copy)
    writes = [
        pltpu.make_async_copy(held.at[n, pl.ds(0, len(group))], outs[n], out_sems.at[n])
        for n, group in enumerate(wanted)
    ]
    for n, write in enumerate(writes):
        for copy in reads[n]:
            copy.wait()
        write.start()
    for write in writes:
        write.wait()


def pack(meta, inputs, wanted):
    hbm = pl.BlockSpec(memory_space=pl.ANY)
    return pl.pallas_call(
        functools.partial(pack_kernel, wanted),
        in_specs=[pl.BlockSpec(memory_space=pltpu.SMEM), hbm],
        out_specs=[hbm] * len(wanted),
        out_shape=[jax.ShapeDtypeStruct((len(group), TOK, 128 * NZ), BF) for group in wanted],
        scratch_shapes=[
            pltpu.VMEM((len(wanted), 2, TOK, 128 * NZ), BF),
            pltpu.SemaphoreType.DMA((len(wanted), 2, NZ)),
            pltpu.SemaphoreType.DMA((len(wanted),)),
        ],
        compiler_params=pltpu.CompilerParams(vmem_limit_bytes=VMEM),
        cost_estimate=pl.CostEstimate(flops=0, bytes_accessed=len(wanted) * 2**22, transcendentals=0),
        name="pack",
    )(meta, inputs)


def product_kernel(token_at, grad_at, n_tokens, n_grads, meta_ref, *refs):
    token_refs, refs = refs[:n_tokens], refs[n_tokens:]
    grad_refs, refs = refs[:n_grads], refs[n_grads:]
    outs, (tokens, grads, acc, token_sems, grad_sems) = refs[:8], refs[8:]
    quarter = acc.shape[0] // 4
    copies = []
    for axis in range(2):
        copies.append([])
        for n in range(8):
            part = pl.ds(n * TOK, TOK)
            ref, index = token_at[axis][n]
            copies[axis].append(
                pltpu.make_async_copy(token_refs[ref].at[index], tokens.at[axis, part], token_sems.at[axis, n])
            )
            ref, index = grad_at[axis][n]
            copies[axis].append(
                pltpu.make_async_copy(grad_refs[ref].at[index], grads.at[axis, :, part], grad_sems.at[axis, n])
            )
        for copy in copies[axis]:
            copy.start()
    for axis in range(2):
        for copy in copies[axis]:
            copy.wait()

        def step(i, carry):
            columns = pl.ds(pl.multiple_of(i * 256, 256), 256)
            acc[...] = dot(grads[axis], tokens[axis, :, columns], 1, 0)
            for away in range(4):
                part = (meta_ref[1 - axis] + away) % 4
                rows = pl.ds(pl.multiple_of(part * quarter, quarter), quarter)
                for z in range(2):
                    outs[4 * axis + away][2 * i + z] = acc[rows, pl.ds(z * 128, 128)].astype(BF)
            return carry

        lax.fori_loop(0, 4, step, 0)


def product(meta, tokens, grads):
    cols = grads[0][0][0].shape[1]
    quarter = cols // 4

    def placed(lists):
        arrays, at = [], []
        for places in lists:
            at.append([])
            for array, index in places:
                known = [n for n, other in enumerate(arrays) if other is array]
                if not known:
                    arrays.append(array)
                at[-1].append((known[0] if known else len(arrays) - 1, index))
        return arrays, at

    token_arrays, token_at = placed(tokens)
    grad_arrays, grad_at = placed(grads)
    hbm = pl.BlockSpec(memory_space=pl.ANY)
    outs = pl.pallas_call(
        functools.partial(product_kernel, token_at, grad_at, len(token_arrays), len(grad_arrays)),
        in_specs=[pl.BlockSpec(memory_space=pltpu.SMEM)] + [hbm] * (len(token_arrays) + len(grad_arrays)),
        out_specs=[pl.BlockSpec(memory_space=pltpu.VMEM)] * 8,
        out_shape=[jax.ShapeDtypeStruct((NZ, quarter, 128), BF)] * 8,
        scratch_shapes=[
            pltpu.VMEM((2, 8 * TOK, 128 * NZ), BF),
            pltpu.VMEM((2, cols, 8 * TOK), BF),
            pltpu.VMEM((cols, 256), F32),
            pltpu.SemaphoreType.DMA((2, 8)),
            pltpu.SemaphoreType.DMA((2, 8)),
        ],
        compiler_params=pltpu.CompilerParams(vmem_limit_bytes=VMEM),
        cost_estimate=pl.CostEstimate(flops=10 * 10**9, bytes_accessed=10 * 2**20, transcendentals=0),
        name="product",
    )(meta, *token_arrays, *grad_arrays)
    return outs[:4], outs[4:]


def total(parts):
    out = parts[0].astype(F32)
    for part in parts[1:]:
        out = out + part.astype(F32)
    return out


def swap(a):
    return lax.ppermute(a, "ctx", CORE)


def send(a, axis, step):
    return lax.ppermute(a, "dp", SHIFTS[axis](step))


STEPS = (1, 3, 2)


def share_pairs(grads):
    chip = jnp.stack([grads, swap(grads)])
    got = [[chip] + [send(chip, axis, step) for step in STEPS] for axis in range(2)]
    return [[(array, core) for array in got[axis] for core in range(2)] for axis in range(2)]


def share_single(grads):
    chip = [grads[None], swap(grads)[None]]
    got = [[send(grads, axis, step) for step in STEPS] for axis in range(2)]
    return [
        [(t, 0) for t in chip] + [(t[None], 0) for part in got[axis] for t in (part, swap(part))]
        for axis in range(2)
    ]


def sum_dp(parts):
    sums = [
        total([parts[axis][0]] + [send(parts[axis][step], 1 - axis, step) for step in STEPS]).astype(BF)
        for axis in range(2)
    ]
    return jnp.stack(sums, axis=1)


Z_GROUPS = [[k + 2 * z for z in range(NZ)] for k in range(2)]


def all_z(a):
    return lax.all_to_all(a, "ctx", split_axis=0, concat_axis=0, axis_index_groups=Z_GROUPS)


def to_all(mine):
    mine = mine.swapaxes(1, 2)
    every = lax.all_to_all(jnp.broadcast_to(mine[None], (16,) + mine.shape), "dp", split_axis=0, concat_axis=0)
    return every.reshape((4, 4) + mine.shape)


def unfold(every):
    first = every[:, :, 0].transpose(0, 2, 1, 3).reshape(512, -1)
    second = every[:, :, 1].transpose(1, 2, 0, 3).reshape(512, -1)
    return jnp.concatenate([first, second], axis=0).astype(F32)


def sum_z(a):
    return jnp.sum(all_z(a).astype(F32), axis=0).astype(BF)


def per_device(queries, key_rows, value_rows, out_grad, inputs, pair_order):
    ctx, dp = lax.axis_index("ctx"), lax.axis_index("dp")
    meta = jnp.stack([dp // 4, dp % 4, ctx % 2, ctx]).astype(jnp.int32)
    me = ctx.reshape(1).astype(jnp.int32)
    own = jnp.concatenate([key_rows[0], value_rows[0]], axis=1)

    wanted = [[((axis, step, 0), (axis, step, 1)) for axis in range(2)] for step in STEPS]
    wanted[2] += [((0, 0, flip), (1, 0, flip)) for flip in range(2)]
    blocks = [own] + [None] * 7
    packed = []
    up = down = own
    for s in range(1, 5):
        up = lax.ppermute(up, "ctx", z_shift(1))
        if s < 4:
            down = lax.ppermute(down, "ctx", z_shift(-1))
            packed.append(pack(meta, inputs[0], wanted[s - 1]))
            up, down, packed, meta = lax.optimization_barrier((up, down, packed, meta))
            blocks[s] = down
        blocks[8 - s] = up
    first = jnp.stack([blocks[dz] for dz in BLOCK_ORDER[0]])
    second = jnp.stack([blocks[dz] for dz in BLOCK_ORDER[1]])
    second, near = lax.optimization_barrier((second, packed[0] + packed[1]))
    blocks = (first, second, swap(first), swap(second))
    near = [send(near[2 * n + axis], axis, step) for n, step in enumerate(STEPS[:2]) for axis in range(2)]

    attn, query_grads, keep, give = attention(me, pair_order, queries[0], out_grad[0], blocks)
    attn, query_grads, keep, give, near, far, mine = lax.optimization_barrier(
        (attn, query_grads, keep, give, near, packed[2][:2], packed[2][2:])
    )
    far = [send(far[axis], axis, STEPS[2]) for axis in range(2)]

    pair = (keep.astype(F32) + swap(give).astype(F32)).astype(BF)
    pair = jnp.roll(pair, ctx // 2, axis=0)
    pair, query_grads = lax.optimization_barrier((pair, query_grads))
    query_grads, far = lax.optimization_barrier((query_grads, far))
    query_grads = share_single(query_grads)
    near_mates = swap(jnp.concatenate([mine[1]] + [part[1:] for part in near]))
    far_mates = swap(jnp.concatenate([part[1:] for part in far]))
    tokens = [
        [(mine[0], axis), (near_mates, axis)]
        + [place for n in range(2) for place in ((near[2 * n + axis], 0), (near_mates, 2 + 2 * n + axis))]
        + [(far[axis], 0), (far_mates, axis)]
        for axis in range(2)
    ]
    kv_grads = share_pairs(sum_z(pair))

    query_sums = sum_dp(product(meta, tokens, query_grads))
    kv_sums = sum_dp(product(meta, tokens, kv_grads))
    every = to_all(sum_z(jnp.concatenate([query_sums, kv_sums], axis=2)))
    weight_grads = jnp.concatenate([unfold(every[..., :128]), unfold(every[..., 128:])], axis=1)
    return attn[None], weight_grads


def solution(mesh):
    rows = P("dp", "ctx", None)
    return jax.shard_map(
        per_device,
        mesh=mesh,
        in_specs=(rows, rows, rows, rows, rows, P()),
        out_specs=(rows, P("ctx", None)),
        check_vma=False,
    )
```

```python
import functools
import math

import jax
import jax.numpy as jnp
from jax import lax
from jax.experimental import pallas as pl
from jax.experimental.pallas import tpu as pltpu
from jax.sharding import PartitionSpec as P

TOK = 256
HALF = 128
HEAD = 128
HEADS = 4
ROWS = HEADS * HALF
NZ = 8
BF = jnp.bfloat16
F32 = jnp.float32
SCALE = 1.0 / math.sqrt(HEAD)
VMEM = 56 * 1024 * 1024

CORE = [(i, i ^ 1) for i in range(16)]


def z_shift(step):
    return [(i, (i + 2 * step) % 16) for i in range(16)]


def x_shift(step):
    return [(i, ((i // 4 + step) % 4) * 4 + i % 4) for i in range(16)]


def y_shift(step):
    return [(i, (i // 4) * 4 + (i % 4 + step) % 4) for i in range(16)]


SHIFTS = (x_shift, y_shift)


def dot(a, b, ca, cb):
    return lax.dot_general(a, b, (((ca,), (cb,)), ((), ())), preferred_element_type=F32)


BLOCK_ORDER = ((0, 1, 7, 2, 6), (3, 5, 4))


def attention_kernel(me_ref, order_ref, q_ref, g_ref, *refs):
    kv_refs, refs = refs[:4], refs[4:]
    attn_ref, qg_ref, keep_ref, send_ref = refs[:4]
    kv, qs, gs, qt, gt, st, extra, mb, lv, acc, rt, sems = refs[4:]
    me = me_ref[0]
    my_z, my_core = me // 2, me % 2
    own = order_ref[me]
    places = [(n, i, dz) for n, order in enumerate(BLOCK_ORDER) for i, dz in enumerate(order)]
    copies = [
        pltpu.make_async_copy(kv_refs[2 * flip + n].at[i], kv.at[NZ * flip + dz], sems.at[flip, dz])
        for flip in range(2)
        for n, i, dz in places
    ]
    for copy in copies:
        copy.start()
    for a in range(2):
        for h in range(HEADS):
            rows, cols, part = pl.ds(a * HALF, HALF), pl.ds(h * HEAD, HEAD), pl.ds(h * HALF, HALF)
            qs[a, part, :] = q_ref[rows, cols]
            gs[a, part, :] = g_ref[rows, cols]
            qt[a, :, part] = q_ref[rows, cols].astype(F32).T.astype(BF)
            gt[a, :, part] = g_ref[rows, cols].astype(F32).T.astype(BF)
    for copy in copies:
        copy.wait()

    def upper(r):
        src = 2 * ((my_z + r % NZ) % NZ) + (my_core + r // NZ) % 2
        return (order_ref[src] > own).astype(jnp.int32)

    def keys(r, half):
        return kv[r, pl.ds(pl.multiple_of(half * HALF, HALF), HALF), :HEAD]

    def values(r, half):
        return kv[r, pl.ds(pl.multiple_of(half * HALF, HALF), HALF), HEAD:]

    def low_keys(dz):
        return jnp.concatenate([keys(dz, 0), keys(NZ + dz, 0)], axis=0)

    def low_values(dz):
        return jnp.concatenate([values(dz, 0), values(NZ + dz, 0)], axis=0)

    def second(dz):
        return ((2, jnp.where(dz == 0, 0, upper(dz)), dz), (3, upper(NZ + dz), NZ + dz))

    causal = (
        lax.broadcasted_iota(jnp.int32, (ROWS, HALF), 0) % HALF
        >= lax.broadcasted_iota(jnp.int32, (ROWS, HALF), 1)
    )
    left, right = pl.ds(0, HALF), pl.ds(HALF, HALF)
    own_high = jnp.where(causal, dot(qs[1], keys(0, 1), 1, 1) * SCALE, -jnp.inf)
    extra[...] = own_high
    mb[0] = jnp.full((ROWS, HEAD), -jnp.inf, F32)
    mb[1] = own_high

    def score_step(dz, carry):
        t0 = dot(qs[1], low_keys(dz), 1, 1) * SCALE
        st[dz, 0], st[dz, 1] = t0[:, :HALF], t0[:, HALF:]
        mb[1] = jnp.maximum(mb[1], jnp.maximum(t0[:, :HALF], t0[:, HALF:]))
        for slot, a, r in second(dz):
            t1 = dot(qs[a], keys(r, a), 1, 1) * SCALE
            if slot == 2:
                t1 = jnp.where(jnp.logical_or(causal, dz > 0), t1, -jnp.inf)
            st[dz, slot] = t1
            mb[a] = jnp.maximum(mb[a], t1)
        return carry

    lax.fori_loop(0, NZ, score_step, 0, unroll=4)
    for a in range(2):
        mb[a] = jnp.broadcast_to(jnp.max(mb[a], axis=1, keepdims=True), (ROWS, HEAD))
    unnorm = jnp.exp(extra[...] - mb[1])
    extra[...] = unnorm
    lv[0] = jnp.zeros((ROWS, HEAD), F32)
    lv[1] = unnorm
    acc[0] = jnp.zeros((ROWS, HEAD), F32)
    acc[1] = dot(unnorm.astype(BF), values(0, 1), 1, 0)

    def forward_step(dz, carry):
        u0 = jnp.exp(st[dz, 0] - mb[1])
        u1 = jnp.exp(st[dz, 1] - mb[1])
        st[dz, 0], st[dz, 1] = u0, u1
        lv[1] += u0 + u1
        acc[1] += dot(jnp.concatenate([u0, u1], axis=1).astype(BF), low_values(dz), 1, 0)
        for slot, a, r in second(dz):
            unnorm = jnp.exp(st[dz, slot] - mb[a])
            st[dz, slot] = unnorm
            lv[a] += unnorm
            acc[a] += dot(unnorm.astype(BF), values(r, a), 1, 0)
        return carry

    lax.fori_loop(0, NZ, forward_step, 0, unroll=4)
    for a in range(2):
        inv = 1.0 / jnp.sum(lv[a], axis=1, keepdims=True)
        out = (acc[a] * inv).astype(BF)
        terms = jnp.sum(gs[a].astype(F32) * out.astype(F32), axis=1, keepdims=True)
        lv[a] = jnp.broadcast_to(inv, (ROWS, HEAD))
        rt[a] = jnp.broadcast_to(terms, (ROWS, HEAD))
        for h in range(HEADS):
            attn_ref[pl.ds(a * HALF, HALF), pl.ds(h * HEAD, HEAD)] = out[h * HALF : (h + 1) * HALF]

    def tile_grads(unnorm, a, r, half):
        probs = unnorm * lv[a]
        prob_grads = dot(gs[a], values(r, half), 1, 1)
        grads = (probs * (prob_grads - rt[a])).astype(BF)
        key_term = dot(qt[a], grads, 1, 0) * SCALE
        value_term = dot(gt[a], probs.astype(BF), 1, 0)
        return grads, jnp.concatenate([key_term, value_term], axis=0)

    grads, high_term = tile_grads(extra[...], 1, 0, 1)
    acc[0] = jnp.zeros((ROWS, HEAD), F32)
    acc[1] = dot(grads, keys(0, 1), 1, 0)
    extra[pl.ds(0, 2 * HEAD), :] = high_term

    def backward_step(dz, carry):
        inv = lv[1]
        terms = rt[1]
        p0, p1 = st[dz, 0] * inv, st[dz, 1] * inv
        prob_grads = dot(gs[1], low_values(dz), 1, 1)
        g0 = p0 * (prob_grads[:, :HALF] - terms)
        g1 = p1 * (prob_grads[:, HALF:] - terms)
        grads = jnp.concatenate([g0, g1], axis=1).astype(BF)
        probs = jnp.concatenate([p0, p1], axis=1).astype(BF)
        acc[1] += dot(grads, low_keys(dz), 1, 0)
        low = jnp.concatenate([dot(qt[1], grads, 1, 0) * SCALE, dot(gt[1], probs, 1, 0)], axis=0)
        for slot, a, r in second(dz):
            grads, term = tile_grads(st[dz, slot], a, r, a)
            acc[a] += dot(grads, keys(r, a), 1, 0)
            out_ref = keep_ref if slot == 2 else send_ref
            here = low[:, :HALF] if slot == 2 else low[:, HALF:]
            above = jnp.where(a == 1, term, 0.0)
            if slot == 2:
                above = jnp.where(dz == 0, extra[pl.ds(0, 2 * HEAD), :], above)
            out_ref[dz, :, left] = (here + jnp.where(a == 0, term, 0.0)).astype(BF)
            out_ref[dz, :, right] = above.astype(BF)
        return carry

    lax.fori_loop(0, NZ, backward_step, 0, unroll=4)
    for a in range(2):
        for h in range(HEADS):
            grad = acc[a, pl.ds(h * HALF, HALF), :] * SCALE
            qg_ref[pl.ds(h * HEAD, HEAD), pl.ds(a * HALF, HALF)] = grad.T.astype(BF)


def attention(me, order, queries, out_grad, blocks):
    smem = pl.BlockSpec(memory_space=pltpu.SMEM)
    vmem = pl.BlockSpec(memory_space=pltpu.VMEM)
    hbm = pl.BlockSpec(memory_space=pl.ANY)
    terms = jax.ShapeDtypeStruct((NZ, 2 * HEAD, TOK), BF)
    stat = pltpu.VMEM((2, ROWS, HEAD), F32)
    return pl.pallas_call(
        attention_kernel,
        in_specs=[smem, smem, vmem, vmem] + [hbm] * 4,
        out_specs=[vmem] * 4,
        out_shape=[
            jax.ShapeDtypeStruct((TOK, HEADS * HEAD), BF),
            jax.ShapeDtypeStruct((HEADS * HEAD, TOK), BF),
            terms,
            terms,
        ],
        scratch_shapes=[
            pltpu.VMEM((16, TOK, 2 * HEAD), BF),
            pltpu.VMEM((2, ROWS, HEAD), BF),
            pltpu.VMEM((2, ROWS, HEAD), BF),
            pltpu.VMEM((2, HEAD, ROWS), BF),
            pltpu.VMEM((2, HEAD, ROWS), BF),
            pltpu.VMEM((NZ, 4, ROWS, HALF), F32),
            pltpu.VMEM((ROWS, HALF), F32),
            stat,
            stat,
            stat,
            stat,
            pltpu.SemaphoreType.DMA((2, NZ)),
        ],
        compiler_params=pltpu.CompilerParams(vmem_limit_bytes=VMEM),
        cost_estimate=pl.CostEstimate(
            flops=22 * 10**9, bytes_accessed=6 * 2**20, transcendentals=33 * ROWS * HALF
        ),
        name="attention",
    )(me, order, queries, out_grad, *blocks)


def pack_kernel(wanted, meta_ref, in_ref, *refs):
    outs, (held, in_sems, out_sems) = refs[:-3], refs[-3:]
    reads = []
    for n, group in enumerate(wanted):
        reads.append([])
        for half, (axis, step, flip) in enumerate(group):
            core = (meta_ref[2] + flip) % 2
            part = (meta_ref[axis] + step) % 4
            for z in range(NZ):
                start = pl.multiple_of((2 * z + core) * 1024 + axis * 512 + part * 128, 128)
                copy = pltpu.make_async_copy(
                    in_ref.at[:, pl.ds(start, 128)],
                    held.at[n, half, :, pl.ds(z * 128, 128)],
                    in_sems.at[n, half, z],
                )
                copy.start()
                reads[n].append(copy)
    writes = [
        pltpu.make_async_copy(held.at[n, pl.ds(0, len(group))], outs[n], out_sems.at[n])
        for n, group in enumerate(wanted)
    ]
    for n, write in enumerate(writes):
        for copy in reads[n]:
            copy.wait()
        write.start()
    for write in writes:
        write.wait()


def pack(meta, inputs, wanted):
    hbm = pl.BlockSpec(memory_space=pl.ANY)
    return pl.pallas_call(
        functools.partial(pack_kernel, wanted),
        in_specs=[pl.BlockSpec(memory_space=pltpu.SMEM), hbm],
        out_specs=[hbm] * len(wanted),
        out_shape=[jax.ShapeDtypeStruct((len(group), TOK, 128 * NZ), BF) for group in wanted],
        scratch_shapes=[
            pltpu.VMEM((len(wanted), 2, TOK, 128 * NZ), BF),
            pltpu.SemaphoreType.DMA((len(wanted), 2, NZ)),
            pltpu.SemaphoreType.DMA((len(wanted),)),
        ],
        compiler_params=pltpu.CompilerParams(vmem_limit_bytes=VMEM),
        cost_estimate=pl.CostEstimate(flops=0, bytes_accessed=len(wanted) * 2**22, transcendentals=0),
        name="pack",
    )(meta, inputs)


def product_kernel(token_at, grad_at, n_tokens, n_grads, meta_ref, *refs):
    token_refs, refs = refs[:n_tokens], refs[n_tokens:]
    grad_refs, refs = refs[:n_grads], refs[n_grads:]
    outs, (tokens, grads, acc, token_sems, grad_sems) = refs[:8], refs[8:]
    quarter = acc.shape[0] // 4
    copies = []
    for axis in range(2):
        copies.append([])
        for n in range(8):
            part = pl.ds(n * TOK, TOK)
            ref, index = token_at[axis][n]
            copies[axis].append(
                pltpu.make_async_copy(token_refs[ref].at[index], tokens.at[axis, part], token_sems.at[axis, n])
            )
            ref, index = grad_at[axis][n]
            copies[axis].append(
                pltpu.make_async_copy(grad_refs[ref].at[index], grads.at[axis, :, part], grad_sems.at[axis, n])
            )
        for copy in copies[axis]:
            copy.start()
    for axis in range(2):
        for copy in copies[axis]:
            copy.wait()

        def step(i, carry):
            columns = pl.ds(pl.multiple_of(i * 256, 256), 256)
            acc[...] = dot(grads[axis], tokens[axis, :, columns], 1, 0)
            for away in range(4):
                part = (meta_ref[1 - axis] + away) % 4
                rows = pl.ds(pl.multiple_of(part * quarter, quarter), quarter)
                for z in range(2):
                    outs[4 * axis + away][2 * i + z] = acc[rows, pl.ds(z * 128, 128)].astype(BF)
            return carry

        lax.fori_loop(0, 4, step, 0)


def product(meta, tokens, grads):
    cols = grads[0][0][0].shape[1]
    quarter = cols // 4

    def placed(lists):
        arrays, at = [], []
        for places in lists:
            at.append([])
            for array, index in places:
                known = [n for n, other in enumerate(arrays) if other is array]
                if not known:
                    arrays.append(array)
                at[-1].append((known[0] if known else len(arrays) - 1, index))
        return arrays, at

    token_arrays, token_at = placed(tokens)
    grad_arrays, grad_at = placed(grads)
    hbm = pl.BlockSpec(memory_space=pl.ANY)
    outs = pl.pallas_call(
        functools.partial(product_kernel, token_at, grad_at, len(token_arrays), len(grad_arrays)),
        in_specs=[pl.BlockSpec(memory_space=pltpu.SMEM)] + [hbm] * (len(token_arrays) + len(grad_arrays)),
        out_specs=[pl.BlockSpec(memory_space=pltpu.VMEM)] * 8,
        out_shape=[jax.ShapeDtypeStruct((NZ, quarter, 128), BF)] * 8,
        scratch_shapes=[
            pltpu.VMEM((2, 8 * TOK, 128 * NZ), BF),
            pltpu.VMEM((2, cols, 8 * TOK), BF),
            pltpu.VMEM((cols, 256), F32),
            pltpu.SemaphoreType.DMA((2, 8)),
            pltpu.SemaphoreType.DMA((2, 8)),
        ],
        compiler_params=pltpu.CompilerParams(vmem_limit_bytes=VMEM),
        cost_estimate=pl.CostEstimate(flops=10 * 10**9, bytes_accessed=10 * 2**20, transcendentals=0),
        name="product",
    )(meta, *token_arrays, *grad_arrays)
    return outs[:4], outs[4:]


def total(parts):
    out = parts[0].astype(F32)
    for part in parts[1:]:
        out = out + part.astype(F32)
    return out


def swap(a):
    return lax.ppermute(a, "ctx", CORE)


def send(a, axis, step):
    return lax.ppermute(a, "dp", SHIFTS[axis](step))


STEPS = (1, 3, 2)


def share_pairs(grads):
    chip = jnp.stack([grads, swap(grads)])
    got = [[chip] + [send(chip, axis, step) for step in STEPS] for axis in range(2)]
    return [[(array, core) for array in got[axis] for core in range(2)] for axis in range(2)]


def share_single(grads):
    chip = [grads[None], swap(grads)[None]]
    got = [[send(grads, axis, step) for step in STEPS] for axis in range(2)]
    return [
        [(t, 0) for t in chip] + [(t[None], 0) for part in got[axis] for t in (part, swap(part))]
        for axis in range(2)
    ]


def sum_dp(parts):
    sums = [
        total([parts[axis][0]] + [send(parts[axis][step], 1 - axis, step) for step in STEPS]).astype(BF)
        for axis in range(2)
    ]
    return jnp.stack(sums, axis=1)


Z_GROUPS = [[k + 2 * z for z in range(NZ)] for k in range(2)]


def all_z(a):
    return lax.all_to_all(a, "ctx", split_axis=0, concat_axis=0, axis_index_groups=Z_GROUPS)


def to_all(mine):
    mine = mine.swapaxes(1, 2)
    every = lax.all_to_all(jnp.broadcast_to(mine[None], (16,) + mine.shape), "dp", split_axis=0, concat_axis=0)
    return every.reshape((4, 4) + mine.shape)


def unfold(every):
    first = every[:, :, 0].transpose(0, 2, 1, 3).reshape(512, -1)
    second = every[:, :, 1].transpose(1, 2, 0, 3).reshape(512, -1)
    return jnp.concatenate([first, second], axis=0).astype(F32)


def sum_z(a):
    return jnp.sum(all_z(a).astype(F32), axis=0).astype(BF)


def per_device(queries, key_rows, value_rows, out_grad, inputs, pair_order):
    ctx, dp = lax.axis_index("ctx"), lax.axis_index("dp")
    meta = jnp.stack([dp // 4, dp % 4, ctx % 2, ctx]).astype(jnp.int32)
    me = ctx.reshape(1).astype(jnp.int32)
    own = jnp.concatenate([key_rows[0], value_rows[0]], axis=1)

    wanted = [[((axis, step, 0), (axis, step, 1)) for axis in range(2)] for step in STEPS]
    wanted[2] += [((0, 0, flip), (1, 0, flip)) for flip in range(2)]
    blocks = [own] + [None] * 7
    packed = []
    up = down = own
    for s in range(1, 5):
        up = lax.ppermute(up, "ctx", z_shift(1))
        if s < 4:
            down = lax.ppermute(down, "ctx", z_shift(-1))
            packed.append(pack(meta, inputs[0], wanted[s - 1]))
            up, down, packed, meta = lax.optimization_barrier((up, down, packed, meta))
            blocks[s] = down
        blocks[8 - s] = up
    first = jnp.stack([blocks[dz] for dz in BLOCK_ORDER[0]])
    second = jnp.stack([blocks[dz] for dz in BLOCK_ORDER[1]])
    second, near = lax.optimization_barrier((second, packed[0] + packed[1]))
    blocks = (first, second, swap(first), swap(second))
    near = [send(near[2 * n + axis], axis, step) for n, step in enumerate(STEPS[:2]) for axis in range(2)]

    attn, query_grads, keep, give = attention(me, pair_order, queries[0], out_grad[0], blocks)
    attn, query_grads, keep, give, near, far, mine = lax.optimization_barrier(
        (attn, query_grads, keep, give, near, packed[2][:2], packed[2][2:])
    )
    far = [send(far[axis], axis, STEPS[2]) for axis in range(2)]

    pair = (keep.astype(F32) + swap(give).astype(F32)).astype(BF)
    pair = jnp.roll(pair, ctx // 2, axis=0)
    pair, query_grads = lax.optimization_barrier((pair, query_grads))
    query_grads = share_single(query_grads)
    near_mates = swap(jnp.concatenate([mine[1]] + [part[1:] for part in near]))
    far_mates = swap(jnp.concatenate([part[1:] for part in far]))
    tokens = [
        [(mine[0], axis), (near_mates, axis)]
        + [place for n in range(2) for place in ((near[2 * n + axis], 0), (near_mates, 2 + 2 * n + axis))]
        + [(far[axis], 0), (far_mates, axis)]
        for axis in range(2)
    ]
    kv_grads = share_pairs(sum_z(pair))

    query_sums = sum_dp(product(meta, tokens, query_grads))
    kv_sums = sum_dp(product(meta, tokens, kv_grads))
    every = to_all(sum_z(jnp.concatenate([query_sums, kv_sums], axis=2)))
    weight_grads = jnp.concatenate([unfold(every[..., :128]), unfold(every[..., 128:])], axis=1)
    return attn[None], weight_grads


def solution(mesh):
    rows = P("dp", "ctx", None)
    return jax.shard_map(
        per_device,
        mesh=mesh,
        in_specs=(rows, rows, rows, rows, rows, P()),
        out_specs=(rows, P("ctx", None)),
        check_vma=False,
    )
```
